32 devices in a mesh: fsdp: 8 (over z, x), tp: 4 (over y, core).
Axes of the slice: x: 2, y: 2, z: 4, core: 2. Of those that a mesh axis runs over, the one named last changes fastest.
Arguments:
- tokens: bfloat16 [4096, 640], P(('fsdp', 'tp')), may hold values from -6 to 6
- sequence_ids: int32 [4096], P(('fsdp', 'tp')), may hold values from 0 to 1, as said below
- positions: int32 [4096], P(('fsdp', 'tp')), may hold values from 0 to 3071, as said below
- query_weight: bfloat16 [640, 1024], P('fsdp', 'tp'), may hold values from -0.25 to 0.25
- key_weight: bfloat16 [640, 256], P('fsdp'), may hold values from -0.25 to 0.25
- value_weight: bfloat16 [640, 256], P('fsdp'), may hold values from -0.25 to 0.25
- project_weight: bfloat16 [1024, 640], P('tp', 'fsdp'), may hold values from -0.1875 to 0.1875
- gate_weight: bfloat16 [640, 2048], P('fsdp', 'tp'), may hold values from -0.25 to 0.25
- up_weight: bfloat16 [640, 2048], P('fsdp', 'tp'), may hold values from -0.25 to 0.25
- down_weight: bfloat16 [2048, 640], P('tp', 'fsdp'), may hold values from -0.125 to 0.125
- prenorm: bfloat16 [640], P('fsdp'), may hold values from 0.25 to 1.75
- postnorm: bfloat16 [640], P('fsdp'), may hold values from 0.25 to 1.75
- midnorm: bfloat16 [640], P('fsdp'), may hold values from 0.25 to 1.75
- endnorm: bfloat16 [640], P('fsdp'), may hold values from 0.25 to 1.75
- querynorm: bfloat16 [256], P('fsdp'), may hold values from 0.25 to 1.75
- keynorm: bfloat16 [256], P('fsdp'), may hold values from 0.25 to 1.75
- cotangent: bfloat16 [4096, 640], P(('fsdp', 'tp')), may hold values from -6 to 6
Outputs:
- layer_out: bfloat16 [4096, 640], P(('fsdp', 'tp'))
- tokens_grad: bfloat16 [4096, 640], P(('fsdp', 'tp'))
- query_grad: float32 [640, 1024], P('fsdp', 'tp')
- key_grad: float32 [640, 256], P('fsdp')
- value_grad: float32 [640, 256], P('fsdp')
- project_grad: float32 [1024, 640], P('tp', 'fsdp')
- gate_grad: float32 [640, 2048], P('fsdp', 'tp')
- up_grad: float32 [640, 2048], P('fsdp', 'tp')
- down_grad: float32 [2048, 640], P('tp', 'fsdp')
- prenorm_grad: float32 [640], P('fsdp')
- postnorm_grad: float32 [640], P('fsdp')
- midnorm_grad: float32 [640], P('fsdp')
- endnorm_grad: float32 [640], P('fsdp')
- querynorm_grad: float32 [256], P('fsdp')
- keynorm_grad: float32 [256], P('fsdp')
The draws below stay inside these ranges and needn't reach their ends.
Inputs may be any that keep to these rules, and one draw needn't show every extreme that they name: sequence_ids never fall along the tokens and rise by one where a sequence begins; every sequence after the first begins inside an aligned block of 512 tokens, never at the block's first token, and every sequence has more than 1024 tokens. `positions`: each token's place in its sequence; places rise by one from token to token within a sequence; every sequence after the first starts at place 0, the first continues a sequence begun before the batch and ends at the largest place.
All inputs are finite; a program needn't handle non-finite values.
Results may differ from the reference program's by a relative error of at most 0.019.
Values may be sent and summed in bfloat16 or wider, within the bound.
A program may use at most 64 MiB of HBM per device.

```python
from functools import partial
import jax
import jax.numpy as jnp
from jax import lax

D = 640
FF = 2048
QH = 4
HD = 256
WINDOW = 512
GROUP = 512
TOKENS = 4096
N_FSDP = 8


def sequence_layout(key):
    start_count = (N_FSDP - 3) // 3
    offsets = jax.random.randint(key, (start_count,), 1, GROUP)
    starts = jnp.arange(1, start_count + 1, dtype=jnp.int32) * (3 * GROUP) + offsets.astype(jnp.int32)
    token_index = jnp.arange(TOKENS, dtype=jnp.int32)
    begun = token_index[:, None] >= starts[None, :]
    numbers = jnp.sum(begun.astype(jnp.int32), axis=1)
    first_anchor = starts[0] - 6 * GROUP
    last_start = jnp.max(jnp.where(begun, starts[None, :], first_anchor), axis=1)
    return (numbers.astype(jnp.int32), (token_index - last_start).astype(jnp.int32))


def draw_sequence_ids(key, part):
    numbers, places = sequence_layout(key)
    return numbers


def draw_positions(key, part):
    numbers, places = sequence_layout(key)
    return places


def block_scale(stream_key, shape, split, least, top_value):
    loudness = 1.0
    for position, shards_of in split:
        steps = jax.random.uniform(jax.random.fold_in(jax.random.fold_in(stream_key, 6), position), (shards_of,), jnp.float32, least / len(split), top_value / len(split))
        loudness = loudness * jnp.repeat(jnp.exp(steps), shape[position] // shards_of).reshape((-1,) + (1,) * (len(shape) - 1 - position))
    return loudness


def centred(own_key, extent, deviation, reach, cuts=(), held_as=jnp.bfloat16):
    values = jax.random.normal(own_key, extent, jnp.float32) * deviation
    if len(cuts) > 0:
        values = block_scale(own_key, extent, cuts, -0.22, 0.18) * values
    return jnp.clip(values, min=-reach, max=reach).astype(held_as)


def setup_inputs(seed: int = 0) -> dict:
    key_of = jax.random.split(jax.random.key(seed), 18)
    return {
        "tokens": centred(key_of[0], (TOKENS, D), 1.0, 6.0, ((0, 32),)),
        "sequence_ids": draw_sequence_ids(jax.random.fold_in(key_of[17], 71), 0),
        "positions": draw_positions(jax.random.fold_in(key_of[17], 71), 0),
        "query_weight": centred(key_of[3], (D, QH * HD), D ** -0.5, 0.25, ((0, 8), (1, 4))),
        "key_weight": centred(key_of[4], (D, HD), D ** -0.5, 0.25, ((0, 8),)),
        "value_weight": centred(key_of[5], (D, HD), D ** -0.5, 0.25, ((0, 8),)),
        "project_weight": centred(key_of[6], (QH * HD, D), (QH * HD) ** -0.5, 0.1875, ((0, 4), (1, 8))),
        "gate_weight": centred(key_of[7], (D, FF), D ** -0.5, 0.25, ((0, 8), (1, 4))),
        "up_weight": centred(key_of[8], (D, FF), D ** -0.5, 0.25, ((0, 8), (1, 4))),
        "down_weight": centred(key_of[9], (FF, D), FF ** -0.5, 0.125, ((0, 4), (1, 8))),
        "prenorm": jnp.clip(1.0 + 0.15 * jax.random.normal(key_of[10], (D,), jnp.float32), 0.25, 1.75).astype(jnp.bfloat16),
        "postnorm": jnp.clip(1.0 + 0.15 * jax.random.normal(key_of[11], (D,), jnp.float32), 0.25, 1.75).astype(jnp.bfloat16),
        "midnorm": jnp.clip(1.0 + 0.15 * jax.random.normal(key_of[12], (D,), jnp.float32), 0.25, 1.75).astype(jnp.bfloat16),
        "endnorm": jnp.clip(1.0 + 0.15 * jax.random.normal(key_of[13], (D,), jnp.float32), 0.25, 1.75).astype(jnp.bfloat16),
        "querynorm": jnp.clip(1.0 + 0.15 * jax.random.normal(key_of[14], (HD,), jnp.float32), 0.25, 1.75).astype(jnp.bfloat16),
        "keynorm": jnp.clip(1.0 + 0.15 * jax.random.normal(key_of[15], (HD,), jnp.float32), 0.25, 1.75).astype(jnp.bfloat16),
        "cotangent": centred(key_of[16], (TOKENS, D), 1.0, 6.0, ((0, 32),)),
    }


@jax.custom_vjp
def low(v):
    return lax.optimization_barrier(v.astype(jnp.bfloat16)).astype(jnp.float32)

@jax.custom_vjp
def low_back(v):
    return v

def low_keep(v):
    return (low(v), None)

def low_pass(kept, grad):
    return (grad,)

def back_keep(v):
    return (v, None)

def back_low(kept, grad):
    return (low(grad),)
low.defvjp(low_keep, low_pass)
low_back.defvjp(back_keep, back_low)
epsilon = 1e-06
rope_base = 10000.0
masked_score = -1e+30

def product(left, right):
    return jnp.dot(left, right, preferred_element_type=jnp.float32, precision=lax.Precision.HIGHEST)

def rms_scale(values, gain_vector):
    return values * lax.rsqrt(lax.optimization_barrier(jnp.mean(values * values, axis=-1, keepdims=True)) + epsilon) * gain_vector

def rotate(values, places):
    half_width = values.shape[-1] // 2
    frequency = rope_base ** (-2.0 * jnp.arange(half_width, dtype=jnp.float32) / values.shape[-1])
    angles = places.astype(jnp.float32)[:, None] * frequency[None, :]
    cosine = jnp.cos(angles)[:, None, :]
    sine_part = jnp.sin(angles)[:, None, :]
    first_half = values[..., :half_width]
    second_half = values[..., half_width:]
    return jnp.concatenate([first_half * cosine - second_half * sine_part, second_half * cosine + first_half * sine_part], axis=-1)

def attention(queries, keys, values, sequence_ids, positions):
    pad_keys = jnp.concatenate([jnp.zeros((WINDOW, HD), keys.dtype), keys], axis=0)
    pad_values = jnp.concatenate([jnp.zeros((WINDOW, HD), values.dtype), values], axis=0)
    pad_marks = jnp.concatenate([jnp.full((WINDOW,), -1, jnp.int32), sequence_ids.astype(jnp.int32)], axis=0)
    pad_places = jnp.concatenate([jnp.zeros((WINDOW,), jnp.int32), positions.astype(jnp.int32)], axis=0)

    def one_block(block_index):
        first_row = (block_index * GROUP).astype(jnp.int32)
        query_block = lax.dynamic_slice_in_dim(queries, first_row, GROUP, 0)
        key_block = lax.dynamic_slice_in_dim(pad_keys, first_row, GROUP + WINDOW, 0)
        value_block = lax.dynamic_slice_in_dim(pad_values, first_row, GROUP + WINDOW, 0)
        query_marks = lax.dynamic_slice_in_dim(sequence_ids.astype(jnp.int32), first_row, GROUP, 0)
        key_marks = lax.dynamic_slice_in_dim(pad_marks, first_row, GROUP + WINDOW, 0)
        query_places = lax.dynamic_slice_in_dim(positions.astype(jnp.int32), first_row, GROUP, 0)
        key_places = lax.dynamic_slice_in_dim(pad_places, first_row, GROUP + WINDOW, 0)
        scores = jnp.einsum('qhd,kd->hqk', query_block, key_block, precision=lax.Precision.HIGHEST) * HD ** (-0.5)
        scores = low_back(scores)
        distance = query_places[:, None] - key_places[None, :]
        allowed = (query_marks[:, None] == key_marks[None, :]) & (distance >= 0) & (distance < WINDOW)
        scores = jnp.where(allowed[None], scores, masked_score)
        attn_probs = low(jax.nn.softmax(scores, axis=-1))
        return jnp.einsum('hqk,kd->qhd', attn_probs, value_block, precision=lax.Precision.HIGHEST)
    blocks = lax.map(jax.checkpoint(one_block), jnp.arange(N_FSDP, dtype=jnp.int32))
    return blocks.reshape(TOKENS, QH * HD)

def forward_layer(sequence_ids, positions, residual, w_query, w_key, w_value, w_project, w_gate, w_up, w_down, gain_pre, gain_post, gain_mid, gain_end, gain_query, gain_key):
    normed = low(rms_scale(residual, gain_pre))
    query_pre = low_back(product(normed, w_query)).reshape(TOKENS, QH, HD)
    key_pre = low_back(product(normed, w_key))
    values = low(low_back(product(normed, w_value)))
    queries = low(rotate(rms_scale(query_pre, gain_query), positions))
    keys = low(rotate(rms_scale(key_pre, gain_key)[:, None, :], positions)[:, 0, :])
    context = low(low_back(attention(queries, keys, values, sequence_ids, positions)))
    attended = low_back(product(context, w_project))
    middle = residual + rms_scale(attended, gain_post)
    mixed = low(rms_scale(middle, gain_mid))
    gate_values = low_back(product(mixed, w_gate))
    up_values = low_back(product(mixed, w_up))
    active = low(jax.nn.gelu(gate_values, approximate=True) * up_values)
    dense_out = low_back(product(active, w_down))
    return middle + rms_scale(dense_out, gain_end)

def reference(tokens, sequence_ids, positions, query_weight, key_weight, value_weight, project_weight, gate_weight, up_weight, down_weight, prenorm, postnorm, midnorm, endnorm, querynorm, keynorm, cotangent):
    inputs = (tokens, query_weight, key_weight, value_weight, project_weight, gate_weight, up_weight, down_weight, prenorm, postnorm, midnorm, endnorm, querynorm, keynorm)
    inputs = tuple((item.astype(jnp.float32) for item in inputs))
    layer = partial(forward_layer, sequence_ids, positions)
    result, pullback = jax.vjp(layer, *inputs)
    grads = pullback(cotangent.astype(jnp.float32))
    return (result.astype(jnp.bfloat16), grads[0].astype(jnp.bfloat16), grads[1], grads[2], grads[3], grads[4], grads[5], grads[6], grads[7], grads[8], grads[9], grads[10], grads[11], grads[12], grads[13])
```

```python
import functools

import jax
import jax.numpy as jnp
from jax import lax
from jax.experimental import pallas as pl
from jax.experimental.pallas import tpu as pltpu
from jax.sharding import PartitionSpec as P

HD = 256
WINDOW = 512
epsilon = 1e-06
rope_base = 10000.0
masked_score = -1e30
f32 = jnp.float32
bf16 = jnp.bfloat16
MESH = pl.DeviceIdType.MESH
VMEM = pl.BlockSpec(memory_space=pltpu.VMEM)
VMEM_LIMIT = 56 * 1024 * 1024


def params(number):
    return pltpu.CompilerParams(
        collective_id=number, has_side_effects=True, vmem_limit_bytes=VMEM_LIMIT
    )


def ring_place(f, n):
    z, x = lax.div(f, 2), lax.rem(f, 2)
    return (1 - x) * z + x * (n - 1 - z)


def ring_member(p, n):
    far = lax.div(p, n // 2)
    return (1 - far) * 2 * p + far * (2 * (n - 1 - p) + 1)


def tp_peers():
    t = lax.axis_index("tp")
    sib = t + 1 - 2 * lax.rem(t, 2)
    far = t + 2 - 4 * lax.div(t, 2)
    opp = sib + 2 - 4 * lax.div(sib, 2)
    return t, sib, far, opp


def greet(ids):
    barrier = pltpu.get_barrier_semaphore()
    for device in ids:
        pl.semaphore_signal(barrier, inc=1, device_id=device, device_id_type=MESH)
    pl.semaphore_wait(barrier, len(ids))


def remote(src, dst, sems, k, device):
    return pltpu.make_async_remote_copy(
        src_ref=src,
        dst_ref=dst,
        send_sem=sems[0].at[k],
        recv_sem=sems[1].at[k],
        device_id=device,
        device_id_type=MESH,
    )


def norm_parts(v, w, g):
    inverse = lax.rsqrt(jnp.mean(v * v, axis=-1, keepdims=True) + epsilon)
    scaled = v * inverse
    u = w * g
    dv = inverse * (u - scaled * jnp.mean(u * scaled, axis=-1, keepdims=True))
    return dv, jnp.sum(w * scaled, axis=0, keepdims=True)


def rms_scale(values, gain_vector):
    return (
        values
        * lax.rsqrt(jnp.mean(values * values, axis=-1, keepdims=True) + epsilon)
        * gain_vector
    )


def gather_kernel(n, directions, count, *refs):
    shards = refs[:count]
    normed_ref, places_ref = refs[count : count + 2]
    outs = refs[count + 2 : 2 * count + 2]
    rows_ref, marks_ref = refs[2 * count + 2 : 2 * count + 4]
    local_sem, send, recv, tp_send, tp_recv = refs[2 * count + 4 :]
    f = lax.axis_index("fsdp")
    p = ring_place(f, n)
    ahead = ring_member(lax.rem(p + 1, n), n)
    behind = ring_member(lax.rem(p - 1 + n, n), n)
    t, sib, far, opp = tp_peers()
    after, before = lax.rem(f + 1, n), lax.rem(f - 1 + n, n)
    greet(
        [
            {"fsdp": ahead},
            {"fsdp": behind},
            {"tp": sib},
            {"tp": far},
            {"fsdp": after},
            {"fsdp": before},
        ]
    )
    locals_ = [pltpu.make_async_copy(s, o.at[f], local_sem.at[k]) for k, (s, o) in enumerate(zip(shards, outs))]
    locals_.append(pltpu.make_async_copy(normed_ref, rows_ref.at[1, t], local_sem.at[count]))
    locals_.append(pltpu.make_async_copy(places_ref, marks_ref.at[1, t], local_sem.at[count + 1]))
    for copy in locals_:
        copy.start()
    pairs = ((normed_ref, rows_ref), (places_ref, marks_ref))
    tp = (tp_send, tp_recv)

    def tp_copy(k, group, slot, device, own=False):
        src, dst = pairs[k % 2]
        return remote(src if own else dst.at[group, slot], dst.at[group, slot], tp, k, device)

    first = []
    for k in range(2):
        src, dst = pairs[k]
        first.append(remote(src, dst.at[0, t], tp, k, {"fsdp": after}))
        first.append(tp_copy(2 + k, 1, t, {"tp": far}, True))
        first.append(tp_copy(4 + k, 1, t, {"tp": sib}, True))
    for copy in first:
        copy.start()

    def ring_copy(s, c):
        if directions[c] == 0:
            slot, device = ring_member(lax.rem(p - s + n, n), n), ahead
        else:
            slot, device = ring_member(lax.rem(p + s, n), n), behind
        src = shards[c] if s == 0 else outs[c].at[slot]
        return remote(src, outs[c].at[slot], (send.at[c], recv.at[c]), s, {"fsdp": device})

    started, latest = [], [None] * count
    for s in range(n - 1):
        for c in range(count):
            if s > 0:
                latest[c].wait_recv()
            latest[c] = ring_copy(s, c)
            latest[c].start()
            started.append(latest[c])
        if s == 0:
            more = []
            for k in range(2):
                first[3 * k].wait_recv()
                more.append(tp_copy(6 + k, 0, t, {"tp": far}))
                more.append(tp_copy(8 + k, 0, t, {"tp": sib}))
            for copy in more:
                copy.start()
            last = []
            for k in range(2):
                first[3 * k + 1].wait_recv()
                last.append(tp_copy(10 + k, 1, far, {"tp": sib}))
            for copy in last:
                copy.start()
        if s == 1:
            for k in range(2):
                more[2 * k].wait_recv()
                last.append(tp_copy(12 + k, 0, far, {"tp": sib}))
                last[-1].start()
    for copy in latest:
        copy.wait_recv()
    for k in range(2):
        first[3 * k + 2].wait_recv()
        more[2 * k + 1].wait_recv()
    for copy in last:
        copy.wait_recv()
    for copy in started + first + more + last:
        copy.wait_send()
    for copy in locals_:
        copy.wait()


def gather_all(n, shards, directions, normed, places):
    count = len(shards)
    outs = [jax.ShapeDtypeStruct((n, *s.shape), s.dtype) for s in shards]
    outs.append(jax.ShapeDtypeStruct((2, 4, *normed.shape), normed.dtype))
    outs.append(jax.ShapeDtypeStruct((2, 4, *places.shape), places.dtype))
    dma = pltpu.SemaphoreType.DMA
    return pl.pallas_call(
        functools.partial(gather_kernel, n, directions, count),
        out_shape=outs,
        in_specs=[VMEM] * (count + 2),
        out_specs=[VMEM] * (count + 2),
        scratch_shapes=[
            dma((count + 2,)),
            dma((count, n - 1)),
            dma((count, n - 1)),
            dma((14,)),
            dma((14,)),
        ],
        compiler_params=params(1),
    )(*shards, normed, places)


def sum_over_tp(part, got, passed, got_far, sems, at):
    t, sib, far, opp = tp_peers()
    a = remote(part.at[opp], got.at[1], sems, at, {"tp": sib})
    b = remote(part.at[sib], got.at[0], sems, at + 1, {"tp": sib})
    a.start()
    b.start()
    a.wait_recv()
    passed[...] = (part[far].astype(f32) + got[1].astype(f32)).astype(bf16)
    c = remote(passed, got_far, sems, at + 2, {"tp": far})
    c.start()
    b.wait_recv()
    total = part[t].astype(f32) + got[0].astype(f32)
    c.wait_recv()
    return total + got_far[...].astype(f32), [a, b, c]


def exchange_kernel(row_math, n_in, n_out, part, *refs):
    row_in = refs[:n_in]
    gathered = refs[n_in]
    row_out = refs[n_in + 1 : n_in + 1 + n_out]
    got, passed, got_far, send, recv = refs[n_in + 1 + n_out :]
    t, sib, far, opp = tp_peers()
    sems = (send, recv)
    greet([{"tp": sib}, {"tp": far}])
    total, sent = sum_over_tp(part, got, passed, got_far, sems, 0)
    gathered[t] = row_math(total, row_in, row_out)
    d = remote(gathered.at[t], gathered.at[t], sems, 3, {"tp": far})
    e = remote(gathered.at[t], gathered.at[t], sems, 4, {"tp": sib})
    d.start()
    e.start()
    d.wait_recv()
    g = remote(gathered.at[far], gathered.at[far], sems, 5, {"tp": sib})
    g.start()
    e.wait_recv()
    g.wait_recv()
    for copy in sent + [d, e, g]:
        copy.wait_send()


def exchange(number, row_math, part, row_in, row_out):
    _, rows, width = part.shape
    dma = pltpu.SemaphoreType.DMA
    return pl.pallas_call(
        functools.partial(exchange_kernel, row_math, len(row_in), len(row_out)),
        out_shape=[jax.ShapeDtypeStruct(part.shape, bf16)]
        + [jax.ShapeDtypeStruct(s, d) for s, d in row_out],
        in_specs=[VMEM] * (1 + len(row_in)),
        out_specs=[VMEM] * (1 + len(row_out)),
        scratch_shapes=[
            pltpu.VMEM((2, rows, width), bf16),
            pltpu.VMEM((rows, width), bf16),
            pltpu.VMEM((rows, width), bf16),
            dma((6,)),
            dma((6,)),
        ],
        compiler_params=params(number),
    )(part, *row_in)


def after_attention(total, row_in, row_out):
    tokens, gain_post, gain_mid = row_in
    attended, middle = row_out
    attended[...] = total
    rows = tokens[...].astype(f32) + rms_scale(total, gain_post[...])
    middle[...] = rows
    return rms_scale(rows, gain_mid[...]).astype(bf16)


def after_dense(total, row_in, row_out):
    middle, cotangent, gain_end = row_in
    layer_out, grad_end = row_out
    layer_out[...] = (middle[...] + rms_scale(total, gain_end[...])).astype(bf16)
    dv, dg = norm_parts(total, cotangent[...].astype(f32), gain_end[...])
    grad_end[...] = dg
    return dv.astype(bf16)


def after_mixed(total, row_in, row_out):
    middle, attended, cotangent, gain_mid, gain_post = row_in
    grad_middle, grad_mid, grad_post = row_out
    dv, dg = norm_parts(middle[...], total, gain_mid[...])
    grad_mid[...] = dg
    rows = cotangent[...].astype(f32) + dv
    grad_middle[...] = rows
    dv, dg = norm_parts(attended[...], rows, gain_post[...])
    grad_post[...] = dg
    return dv.astype(bf16)


def back_kernel(n, width, part, normed_out, pair_out, got, passed, got_far, low, landed, send, recv):
    t, sib, far, opp = tp_peers()
    f = lax.axis_index("fsdp")
    after, before = lax.rem(f + 1, n), lax.rem(f - 1 + n, n)
    greet([{"tp": sib}, {"tp": far}, {"fsdp": after}, {"fsdp": before}])
    sems = (send, recv)
    total, sent = sum_over_tp(part, got, passed, got_far, sems, 0)
    low[...] = total[:, width + 2 * HD :].astype(bf16)
    back = remote(low, landed, sems, 3, {"fsdp": before})
    back.start()
    normed_out[...] = total[:, :width]
    back.wait_recv()
    keep = jnp.where(f < n - 1, 1.0, 0.0).astype(f32)
    pair_out[...] = total[:, width : width + 2 * HD] + landed[...].astype(f32) * keep
    for copy in sent + [back]:
        copy.wait_send()


def send_back(n, part, width):
    _, rows, whole = part.shape
    dma = pltpu.SemaphoreType.DMA
    return pl.pallas_call(
        functools.partial(back_kernel, n, width),
        out_shape=[
            jax.ShapeDtypeStruct((rows, width), f32),
            jax.ShapeDtypeStruct((rows, 2 * HD), f32),
        ],
        in_specs=[VMEM],
        out_specs=[VMEM] * 2,
        scratch_shapes=[
            pltpu.VMEM((2, rows, whole), bf16),
            pltpu.VMEM((rows, whole), bf16),
            pltpu.VMEM((rows, whole), bf16),
            pltpu.VMEM((rows, 2 * HD), bf16),
            pltpu.VMEM((rows, 2 * HD), bf16),
            dma((4,)),
            dma((4,)),
        ],
        compiler_params=params(5),
    )(part)


def reduce_kernel(n, directions, shared, count, *refs):
    grads = refs[:count]
    outs = refs[count : 2 * count]
    lands = refs[2 * count : 3 * count]
    own_parts = refs[3 * count : 3 * count + shared]
    tp_lands = refs[3 * count + shared : 3 * count + 2 * shared]
    send, recv, tp_send, tp_recv = refs[3 * count + 2 * shared :]
    f = lax.axis_index("fsdp")
    p = ring_place(f, n)
    ahead = ring_member(lax.rem(p + 1, n), n)
    behind = ring_member(lax.rem(p - 1 + n, n), n)
    t, sib, far, opp = tp_peers()
    peers = [{"tp": sib}, {"tp": far}, {"tp": opp}]
    greet([{"fsdp": ahead}, {"fsdp": behind}] + peers)

    def block(s, c):
        q = lax.rem(p - 1 - s + 2 * n, n) if directions[c] == 0 else lax.rem(p + 1 + s, n)
        return ring_member(q, n)

    started, latest = [], [None] * count
    for s in range(n - 1):
        for c in range(count):
            src = grads[c].at[block(s, c)]
            if s > 0:
                latest[c].wait_recv()
                land = lands[c]
                land[s - 1] = (
                    land[s - 1].astype(f32) + grads[c][block(s, c)].astype(f32)
                ).astype(bf16)
                src = land.at[s - 1]
            device = ahead if directions[c] == 0 else behind
            latest[c] = remote(
                src, lands[c].at[s], (send.at[c], recv.at[c]), s, {"fsdp": device}
            )
            latest[c].start()
            started.append(latest[c])
    tp_copies = []
    for c in range(count):
        latest[c].wait_recv()
        total = lands[c][n - 2].astype(f32) + grads[c][f].astype(f32)
        outs[c][...] = total
        if c < shared:
            own_parts[c][...] = total.astype(bf16)
            for k, peer in enumerate(peers):
                copy = remote(
                    own_parts[c], tp_lands[c].at[k], (tp_send.at[c], tp_recv.at[c]), k, peer
                )
                copy.start()
                tp_copies.append(copy)
    for c in range(shared):
        for k in range(3):
            tp_copies[3 * c + k].wait_recv()
        outs[c][...] = (
            outs[c][...]
            + tp_lands[c][0].astype(f32)
            + tp_lands[c][1].astype(f32)
            + tp_lands[c][2].astype(f32)
        )
    for copy in started + tp_copies:
        copy.wait_send()


def reduce_all(n, grads, directions, shared):
    count = len(grads)
    shapes = [g.shape[1:] for g in grads]
    dma = pltpu.SemaphoreType.DMA
    return pl.pallas_call(
        functools.partial(reduce_kernel, n, directions, shared, count),
        out_shape=[jax.ShapeDtypeStruct(s, f32) for s in shapes],
        in_specs=[VMEM] * count,
        out_specs=[VMEM] * count,
        scratch_shapes=[pltpu.VMEM((n - 1, *s), bf16) for s in shapes]
        + [pltpu.VMEM(s, bf16) for s in shapes[:shared]]
        + [pltpu.VMEM((3, *s), bf16) for s in shapes[:shared]]
        + [dma((count, n - 1)), dma((count, n - 1)), dma((shared, 3)), dma((shared, 3))],
        compiler_params=params(6),
    )(*grads)


def angles_of(places):
    half = HD // 2
    frequency = rope_base ** (-2.0 * jnp.arange(half, dtype=f32) / HD)
    angles = places.astype(f32)[:, None] * frequency[None, :]
    return jnp.cos(angles), jnp.sin(angles)


def rotate(v, cos, sin):
    a, b = v[:, : HD // 2], v[:, HD // 2 :]
    return jnp.concatenate([a * cos - b * sin, b * cos + a * sin], axis=-1)


def rotate_back(v, cos, sin):
    a, b = v[:, : HD // 2], v[:, HD // 2 :]
    return jnp.concatenate([a * cos + b * sin, b * cos - a * sin], axis=-1)


def dot(a, b, da, db):
    return lax.dot_general(a, b, (((da,), (db,)), ((), ())), preferred_element_type=f32)


def gated_gelu(gate_values, up_values):
    return jax.nn.gelu(gate_values, approximate=True) * up_values


def per_device(
    n,
    tokens,
    sequence_ids,
    positions,
    query_weight,
    key_weight,
    value_weight,
    project_weight,
    gate_weight,
    up_weight,
    down_weight,
    prenorm,
    postnorm,
    midnorm,
    endnorm,
    querynorm,
    keynorm,
    cotangent,
):
    rows, width = tokens.shape
    part = query_weight.shape[0]
    padded = -(-part // 16) * 16
    small = querynorm.shape[0]

    def pad_rows(a):
        return jnp.pad(a, ((0, padded - a.shape[0]), (0, 0))) if a.shape[0] < padded else a

    gains = jnp.stack([prenorm, postnorm, midnorm, endnorm], axis=1)
    head_gains = jnp.stack([querynorm, keynorm], axis=1)
    extra = jnp.pad(gains, ((0, padded - part), (0, 124))) + jnp.pad(
        head_gains, ((0, padded - small), (4, 122))
    )
    shards = [
        pad_rows(query_weight),
        pad_rows(key_weight),
        extra,
        pad_rows(value_weight),
        pad_rows(project_weight.T),
        pad_rows(gate_weight),
        pad_rows(up_weight),
        pad_rows(down_weight.T),
    ]
    directions = (0, 1, 0, 1, 1, 0, 1, 0)
    residual = tokens.astype(f32)
    scaled = residual * lax.rsqrt(jnp.mean(residual * residual, axis=-1, keepdims=True) + epsilon)
    gain_pre_whole = lax.all_gather(prenorm, "fsdp", axis=0, tiled=True).astype(f32)
    normed_own = (scaled * gain_pre_whole).astype(bf16)
    place_block = jnp.broadcast_to(positions[None, :], (8, rows))
    *full, normed_pair, places_pair = gather_all(n, shards, directions, normed_own, place_block)
    full = [a[:, :part].reshape(n * part, a.shape[2]) for a in full]
    w_query, w_key, extra_all, w_value, w_project, w_gate, w_up, w_down = full
    gain_rows = extra_all[:, :4].astype(f32).T
    gain_post, gain_mid, gain_end = gain_rows[1:2], gain_rows[2:3], gain_rows[3:4]
    head_rows = (
        extra_all.reshape(n, part, 128)[:, :small, 4:6].reshape(n * small, 2).astype(f32).T
    )
    gain_query, gain_key = head_rows[0:1], head_rows[1:2]

    group = 4 * rows
    first = lax.axis_index("fsdp") == 0
    normed_ext = normed_pair.reshape(2 * group, width)
    normed_group = normed_ext[group:]
    places_ext = places_pair[:, :, 0, :].reshape(2 * group)
    places_group = places_ext[group:]
    cos_ext, sin_ext = angles_of(places_ext)
    cos, sin = cos_ext[group:], sin_ext[group:]
    query_pre = dot(normed_group, w_query, 1, 0)
    key_pre = dot(normed_ext, w_key, 1, 0)
    values = dot(normed_ext, w_value, 1, 0).astype(bf16)
    queries = rotate(rms_scale(query_pre, gain_query), cos, sin).astype(bf16)
    keys = rotate(rms_scale(key_pre, gain_key), cos_ext, sin_ext).astype(bf16)

    apart = (jnp.arange(group, dtype=jnp.int32) + group)[:, None] - jnp.arange(
        2 * group, dtype=jnp.int32
    )[None, :]
    reach = jnp.minimum(places_group, WINDOW - 1)
    reach = jnp.where(first, jnp.minimum(reach, jnp.arange(group, dtype=jnp.int32)), reach)
    allowed = (apart >= 0) & (apart <= reach[:, None])
    score_scale = HD ** (-0.5)
    scores = jnp.where(allowed, dot(queries, keys, 1, 1) * score_scale, masked_score)
    exponent = jnp.exp(scores - jnp.max(scores, axis=-1, keepdims=True))
    weights = exponent / jnp.sum(exponent, axis=-1, keepdims=True)
    probs = weights.astype(bf16)
    context = dot(probs, values, 1, 0).astype(bf16)
    attended_part = dot(context, w_project, 1, 1).astype(bf16).reshape(4, rows, width)
    row_f32 = ((rows, width), f32)
    gain_out = ((1, width), f32)
    mixed, attended, middle = exchange(
        2, after_attention, attended_part, [tokens, gain_post, gain_mid], [row_f32, row_f32]
    )
    mixed = mixed.reshape(group, width)
    gate_values = dot(mixed, w_gate, 1, 0)
    up_values = dot(mixed, w_up, 1, 0)
    active = gated_gelu(gate_values, up_values).astype(bf16)
    dense_part = dot(active, w_down, 1, 1).astype(bf16).reshape(4, rows, width)
    grad_dense, layer_out, grad_end = exchange(
        3,
        after_dense,
        dense_part,
        [middle, cotangent, gain_end],
        [((rows, width), bf16), gain_out],
    )
    grad_dense = grad_dense.reshape(group, width)
    grad_active = dot(grad_dense, w_down, 1, 0)
    grad_wdown = dot(grad_dense, active, 0, 0).astype(bf16)
    _, gelu_back = jax.vjp(gated_gelu, gate_values, up_values)
    grad_gate, grad_up = gelu_back(grad_active)
    grad_gate, grad_up = grad_gate.astype(bf16), grad_up.astype(bf16)
    grad_wgate = dot(mixed, grad_gate, 0, 0).astype(bf16)
    grad_wup = dot(mixed, grad_up, 0, 0).astype(bf16)
    mixed_part = (dot(grad_gate, w_gate, 1, 1) + dot(grad_up, w_up, 1, 1)).astype(bf16)
    grad_attended, grad_middle, grad_mid, grad_post = exchange(
        4,
        after_mixed,
        mixed_part.reshape(4, rows, width),
        [middle, attended, cotangent, gain_mid, gain_post],
        [row_f32, gain_out, gain_out],
    )
    grad_attended = grad_attended.reshape(group, width)
    grad_wproject = dot(grad_attended, context, 0, 0).astype(bf16)
    grad_context = dot(grad_attended, w_project, 1, 0).astype(bf16)
    grad_probs = dot(grad_context, values, 1, 1)
    inner = jnp.sum(weights * grad_probs, axis=-1, keepdims=True)
    grad_scores = (weights * (grad_probs - inner)).astype(bf16)
    grad_queries = dot(grad_scores, keys, 1, 0) * score_scale
    grad_keys = (dot(grad_scores, queries, 0, 0) * score_scale).astype(bf16)
    grad_values = dot(probs, grad_context, 0, 0).astype(bf16)
    grad_query_pre, grad_qgain = norm_parts(
        query_pre, rotate_back(grad_queries, cos, sin), gain_query
    )
    grad_query_low = grad_query_pre.astype(bf16)
    grad_wquery = dot(normed_group, grad_query_low, 0, 0).astype(bf16)
    normed_part = dot(grad_query_low, w_query, 1, 1).astype(bf16)
    back_part = jnp.concatenate(
        [
            normed_part,
            grad_keys[group:],
            grad_values[group:],
            grad_keys[:group],
            grad_values[:group],
        ],
        axis=1,
    ).reshape(4, rows, width + 4 * HD)
    grad_normed, grad_pair = send_back(n, back_part, width)
    own = lax.axis_index("tp") * rows
    key_pre_own = lax.dynamic_slice_in_dim(key_pre, group + own, rows, 0)
    cos_own = lax.dynamic_slice_in_dim(cos, own, rows, 0)
    sin_own = lax.dynamic_slice_in_dim(sin, own, rows, 0)
    grad_key_pre, grad_kgain = norm_parts(
        key_pre_own, rotate_back(grad_pair[:, :HD], cos_own, sin_own), gain_key
    )
    grad_key_low = grad_key_pre.astype(bf16)
    grad_value_low = grad_pair[:, HD:].astype(bf16)
    grad_wkey = dot(normed_own, grad_key_low, 0, 0).astype(bf16)
    grad_wvalue = dot(normed_own, grad_value_low, 0, 0).astype(bf16)
    grad_normed = (
        grad_normed + dot(grad_key_low, w_key, 1, 1) + dot(grad_value_low, w_value, 1, 1)
    )
    grad_residual, grad_pre = norm_parts(residual, grad_normed, gain_pre_whole[None, :])
    tokens_grad = (grad_middle + grad_residual).astype(bf16)

    def blocks(g):
        g = g.reshape(n, part, g.shape[1])
        return jnp.pad(g, ((0, 0), (0, padded - part), (0, 0))) if part < padded else g

    gain_grads = jnp.concatenate([grad_pre, grad_post, grad_mid, grad_end], axis=0).T
    gain_grads = gain_grads.reshape(n, part, 4)
    head_grads = jnp.concatenate([grad_qgain, grad_kgain], axis=0).T.reshape(n, small, 2)
    extra_grads = (
        jnp.pad(gain_grads, ((0, 0), (0, padded - part), (0, 124)))
        + jnp.pad(head_grads, ((0, 0), (0, padded - small), (4, 122)))
    ).astype(bf16)
    sums = reduce_all(
        n,
        [
            blocks(grad_wkey),
            blocks(grad_wvalue),
            extra_grads,
            blocks(grad_wquery),
            blocks(grad_wproject),
            blocks(grad_wgate),
            blocks(grad_wup),
            blocks(grad_wdown),
        ],
        (1, 0, 0, 0, 1, 0, 1, 1),
        3,
    )
    sums = [s[:part] for s in sums]
    s_key, s_value, s_extra, s_query, s_project, s_gate, s_up, s_down = sums
    return (
        layer_out,
        tokens_grad,
        s_query,
        s_key,
        s_value,
        s_project.T,
        s_gate,
        s_up,
        s_down.T,
        s_extra[:, 0],
        s_extra[:, 1],
        s_extra[:, 2],
        s_extra[:, 3],
        s_extra[:small, 4],
        s_extra[:small, 5],
    )


def solution(mesh):
    rows = P(("fsdp", "tp"), None)
    marks = P(("fsdp", "tp"))
    both, down, across, gain = P("fsdp", "tp"), P("fsdp", None), P("tp", "fsdp"), P("fsdp")
    return jax.shard_map(
        functools.partial(per_device, mesh.shape["fsdp"]),
        mesh=mesh,
        in_specs=(rows, marks, marks, both, down, down, across, both, both, across)
        + (gain,) * 6
        + (rows,),
        out_specs=(rows, rows, both, down, down, across, both, both, across) + (gain,) * 6,
        check_vma=False,
    )
```

```python
import functools

import jax
import jax.numpy as jnp
import numpy as np
from jax import lax
from jax.experimental import pallas as pl
from jax.experimental.pallas import tpu as pltpu
from jax.sharding import PartitionSpec as P

HD = 256
WINDOW = 512
epsilon = 1e-06
rope_base = 10000.0
masked_score = -1e30
f32 = jnp.float32
bf16 = jnp.bfloat16
MESH = pl.DeviceIdType.MESH
VMEM = pl.BlockSpec(memory_space=pltpu.VMEM)
GELU = 0.7978845608028654
VMEM_LIMIT = 56 * 1024 * 1024


def params(number):
    return pltpu.CompilerParams(
        collective_id=number, has_side_effects=True, vmem_limit_bytes=VMEM_LIMIT
    )


def ring_place(f, n):
    z, x = lax.div(f, 2), lax.rem(f, 2)
    return (1 - x) * z + x * (n - 1 - z)


def ring_member(p, n):
    far = lax.div(p, n // 2)
    return (1 - far) * 2 * p + far * (2 * (n - 1 - p) + 1)


def tp_peers():
    t = lax.axis_index("tp")
    sib = t + 1 - 2 * lax.rem(t, 2)
    far = t + 2 - 4 * lax.div(t, 2)
    opp = sib + 2 - 4 * lax.div(sib, 2)
    return t, sib, far, opp


def greet(ids):
    barrier = pltpu.get_barrier_semaphore()
    for device in ids:
        pl.semaphore_signal(barrier, inc=1, device_id=device, device_id_type=MESH)
    pl.semaphore_wait(barrier, len(ids))


def remote(src, dst, sems, k, device):
    return pltpu.make_async_remote_copy(
        src_ref=src,
        dst_ref=dst,
        send_sem=sems[0].at[k],
        recv_sem=sems[1].at[k],
        device_id=device,
        device_id_type=MESH,
    )


def inverse_scale(v, width):
    return lax.rsqrt(jnp.sum(v * v, axis=-1, keepdims=True) * (1.0 / width) + epsilon)


def norm_parts(v, w, g, width):
    inverse = inverse_scale(v, width)
    scaled = v * inverse
    u = w * g
    dv = inverse * (u - scaled * (jnp.sum(u * scaled, axis=-1, keepdims=True) * (1.0 / width)))
    return dv, jnp.sum(w * scaled, axis=0, keepdims=True)


def dot(a, b, da, db):
    return lax.dot_general(a, b, (((da,), (db,)), ((), ())), preferred_element_type=f32)


def rotate(v, cos, sin):
    a, b = v[:, : HD // 2], v[:, HD // 2 :]
    return jnp.concatenate([a * cos - b * sin, b * cos + a * sin], axis=-1)


def rotate_back(v, cos, sin):
    a, b = v[:, : HD // 2], v[:, HD // 2 :]
    return jnp.concatenate([a * cos + b * sin, b * cos - a * sin], axis=-1)


def iota(shape, dim):
    return lax.broadcasted_iota(jnp.int32, shape, dim)


def spread(pieces, n, each, columns):
    pick = (lax.rem(iota((128, columns), 1), each) == iota((128, columns), 0)).astype(bf16)
    laid = dot(pieces, pick, 1, 0)
    laid = jnp.where(
        lax.div(iota(laid.shape, 0), 16) == lax.div(iota(laid.shape, 1), each), laid, 0.0
    )
    return jnp.sum(laid.reshape(n, 16, columns), axis=0)


FETCH_WAY = dict(query=0, key=1, value=0, project=1, gate=0, up=1, down=0)
SUM_WAY = dict(gate=0, up=1, down=0, project=1, query=0, key=1, value=1, extra=0)
WEIGHTS = tuple(FETCH_WAY)
EARLY, LATE = WEIGHTS[:4], WEIGHTS[4:]
SHARED = ("key", "value")
TWICE = ("extra",) + SHARED
NEXT = ("query", "project") + LATE


class Fetch:
    def __init__(self, n, p, hop, shard, whole, sems, way):
        self.n, self.p, self.hop, self.shard, self.whole = n, p, hop, shard, whole
        self.sems, self.way, self.step, self.sent = sems, way, 0, []

    def advance(self):
        s, n = self.step, self.n
        if s > n - 1:
            return
        if s > 0:
            self.sent[-1].wait_recv()
        if s < n - 1:
            q = lax.rem(self.p - s + n, n) if self.way == 0 else lax.rem(self.p + s, n)
            slot = self.whole.at[ring_member(q, n)]
            src = self.shard if s == 0 else slot
            copy = remote(src, slot, self.sems, s, dict(fsdp=self.hop[self.way]))
            copy.start()
            self.sent.append(copy)
        self.step += 1


class Collect:
    def __init__(self, n, p, hop, grads, land, sems, way):
        self.n, self.p, self.hop, self.grads, self.land = n, p, hop, grads, land
        self.sems, self.way, self.step, self.sent = sems, way, 0, []

    def advance(self):
        s, n, land = self.step, self.n, self.land
        if s > n - 2:
            return
        q = lax.rem(self.p - 1 - s + 2 * n, n) if self.way == 0 else lax.rem(self.p + 1 + s, n)
        slot = ring_member(q, n)
        src = self.grads.at[slot]
        if s > 0:
            self.sent[-1].wait_recv()
            land[s - 1] = (land[s - 1].astype(f32) + self.grads[slot].astype(f32)).astype(bf16)
            src = land.at[s - 1]
        copy = remote(src, land.at[s], self.sems, s, dict(fsdp=self.hop[self.way]))
        copy.start()
        self.sent.append(copy)
        self.step += 1

    def finish(self, f):
        while self.step < self.n - 1:
            self.advance()
        self.sent[-1].wait_recv()
        return self.land[self.n - 2].astype(f32) + self.grads[f].astype(f32)


class Refs:
    pass


def layer_kernel(n, width, small, names, *refs):
    r = Refs()
    for name, ref in zip(names, refs):
        setattr(r, name, ref)
    f = lax.axis_index("fsdp")
    p = ring_place(f, n)
    hop = (ring_member(lax.rem(p + 1, n), n), ring_member(lax.rem(p - 1 + n, n), n))
    t, sib, far, opp = tp_peers()
    after, before = lax.rem(f + 1, n), lax.rem(f - 1 + n, n)
    others = [lax.rem(f + d, n) for d in range(1, n)]
    greet(
        [dict(fsdp=device) for device in others] + [dict(tp=sib), dict(tp=far), dict(tp=opp)]
    )
    tp, used, unsent, local = (r.tp_send, r.tp_recv), [0], [], []

    def start(src, dst, device):
        copy = remote(src, dst, tp, used[0], device)
        used[0] += 1
        copy.start()
        unsent.append(copy)
        return copy

    fetch = {}
    for k, name in enumerate(WEIGHTS):
        shard, whole = getattr(r, "s_" + name), getattr(r, "w_" + name)
        fetch[name] = Fetch(
            n, p, hop, shard, whole, (r.fetch_send.at[k], r.fetch_recv.at[k]), FETCH_WAY[name]
        )
    collect = {}
    for k, name in enumerate(SUM_WAY):
        collect[name] = Collect(
            n,
            p,
            hop,
            getattr(r, "g_" + name),
            getattr(r, "land_" + name),
            (r.sum_send.at[k], r.sum_recv.at[k]),
            SUM_WAY[name],
        )

    def fetch_on(*which):
        for name in which:
            fetch[name].advance()

    def collect_on(*which):
        for name in which:
            collect[name].advance()

    moves = [(r.gains, r.all_gains.at[f]), (r.places, r.marks.at[t])]
    moves += [(getattr(r, "s_" + name), getattr(r, "w_" + name).at[f]) for name in WEIGHTS]
    for k, (src, dst) in enumerate(moves):
        local.append(pltpu.make_async_copy(src, dst, r.local_sem.at[k]))
        local[-1].start()
    gain_copies = []
    for k, device in enumerate(others):
        copy = remote(
            r.gains, r.all_gains.at[f], (r.gain_send, r.gain_recv), k, dict(fsdp=device)
        )
        copy.start()
        gain_copies.append(copy)
    mark_copies = [
        start(r.places, r.marks.at[t], dict(tp=peer)) for peer in (sib, far, opp)
    ]
    fetch_on(*EARLY)
    tokens = r.tokens[...].astype(f32)
    scaled = tokens * inverse_scale(tokens, width)
    local[0].wait()
    for copy in gain_copies:
        copy.wait_recv()
    pieces = r.all_gains[...].reshape(n * 16, 128)
    wide = tokens.shape[1]
    gains = spread(pieces, n, wide // n, wide)
    head_gains = spread(pieces, n, small, HD)
    gain_pre, gain_post, gain_mid, gain_end = (gains[k : k + 1] for k in range(4))
    gain_query, gain_key = head_gains[4:5], head_gains[5:6]
    r.normed[4 + t] = (scaled * gain_pre).astype(bf16)
    own = r.normed.at[4 + t]
    to_next = start(own, r.normed.at[t], dict(fsdp=after))
    to_far = start(own, own, dict(tp=far))
    to_sib = start(own, own, dict(tp=sib))
    fetch_on(*EARLY)
    to_far.wait_recv()
    far_sib = start(r.normed.at[4 + far], r.normed.at[4 + far], dict(tp=sib))
    fetch_on(*EARLY)
    to_next.wait_recv()
    prev = r.normed.at[t]
    prev_far = start(prev, prev, dict(tp=far))
    prev_sib = start(prev, prev, dict(tp=sib))
    fetch_on(*EARLY)
    prev_far.wait_recv()
    prev_far_sib = start(r.normed.at[far], r.normed.at[far], dict(tp=sib))
    for s in range(4, n):
        fetch_on(*EARLY)
        if s == 4:
            fetch_on(*LATE)
    for copy in [to_sib, far_sib, prev_sib, prev_far_sib] + mark_copies:
        copy.wait_recv()
    for copy in local[1:]:
        copy.wait()

    def whole(name):
        ref = getattr(r, "w_" + name)
        return ref[...].reshape(wide, ref.shape[2])

    w_query, w_key, w_value = whole("query"), whole("key"), whole("value")

    def key_block(b, carry):
        rows = r.normed[b]
        key_pre = dot(rows, w_key, 1, 0)
        r.key_pre[b] = key_pre
        scaled_key = key_pre * inverse_scale(key_pre, HD) * gain_key
        place = pl.ds(pl.multiple_of(b * 128, 128), 128)
        r.keys[place, :] = rotate(scaled_key, r.cos[b], r.sin[b]).astype(bf16)
        r.values[place, :] = dot(rows, w_value, 1, 0).astype(bf16)
        return carry

    lax.fori_loop(0, 8, key_block, 0)
    fetch_on(*LATE)
    score_scale = HD ** (-0.5)
    for b in range(4):
        query_pre = dot(r.normed[4 + b], w_query, 1, 0)
        r.query_pre[b] = query_pre
        scaled_query = query_pre * inverse_scale(query_pre, HD) * gain_query
        queries = rotate(scaled_query, r.cos[4 + b], r.sin[4 + b]).astype(bf16)
        r.queries[b] = queries
        window = slice(128 * b, 128 * b + 128 + WINDOW)
        scores = dot(queries, r.keys[window, :], 1, 1) * score_scale
        places = jnp.broadcast_to(r.marks[b][0:1, :], (128, 128)).astype(f32)
        reach = jnp.minimum(jnp.transpose(places)[:, 0:1], WINDOW - 1.0)
        limit = iota((128, 1), 0) + (128 * b + f * 8192)
        reach = jnp.minimum(reach, limit.astype(f32))
        apart = (WINDOW + iota(scores.shape, 0) - iota(scores.shape, 1)).astype(f32)
        scores = jnp.where((apart >= 0) & (apart <= reach), scores, masked_score)
        exponent = jnp.exp(scores - jnp.max(scores, axis=-1, keepdims=True))
        weights = exponent * (1.0 / jnp.sum(exponent, axis=-1, keepdims=True))
        r.weights[b] = weights
        r.context[b] = dot(weights.astype(bf16), r.values[window, :], 1, 0).astype(bf16)
        if b % 2 == 1:
            fetch_on(*LATE)
    w_project = whole("project")
    for b in range(4):
        r.part_a[b] = dot(r.context[b], w_project, 1, 1).astype(bf16)

    def sum_rows(part, got, passed, got_far, beside=()):
        a = start(part.at[opp], got.at[1], dict(tp=sib))
        b = start(part.at[sib], got.at[0], dict(tp=sib))
        if len(beside) > 0:
            beside[0]()
        a.wait_recv()
        passed[...] = (part[far].astype(f32) + got[1].astype(f32)).astype(bf16)
        c = start(passed, got_far, dict(tp=far))
        if len(beside) > 1:
            beside[1]()
        b.wait_recv()
        total = part[t].astype(f32) + got[0].astype(f32)
        c.wait_recv()
        return total + got_far[...].astype(f32)

    def gather_rows(gathered, rows, beside=None):
        gathered[t] = rows
        own = gathered.at[t]
        d = start(own, own, dict(tp=far))
        e = start(own, own, dict(tp=sib))
        if beside is not None:
            beside()
        d.wait_recv()
        g = start(gathered.at[far], gathered.at[far], dict(tp=sib))
        e.wait_recv()
        g.wait_recv()

    def fetch_mlp():
        fetch_on(*LATE)

    attended = sum_rows(r.part_a, r.got_a, r.passed_a, r.far_a, (fetch_mlp, fetch_mlp))
    r.attended[...] = attended
    middle = tokens + attended * inverse_scale(attended, width) * gain_post
    r.middle[...] = middle
    mixed_own = (middle * inverse_scale(middle, width) * gain_mid).astype(bf16)
    gather_rows(r.mixed, mixed_own, fetch_mlp)
    for s in range(n):
        fetch_mlp()
    w_gate, w_up, w_down = whole("gate"), whole("up"), whole("down")
    for b in range(4):
        gate_values = dot(r.mixed[b], w_gate, 1, 0)
        up_values = dot(r.mixed[b], w_up, 1, 0)
        inner = jnp.tanh(
            GELU * (gate_values + 0.044715 * gate_values * gate_values * gate_values)
        )
        gelu = 0.5 * gate_values * (1.0 + inner)
        slope = 0.5 * (1.0 + inner) + 0.5 * gate_values * (1.0 - inner * inner) * GELU * (
            1.0 + 3 * 0.044715 * gate_values * gate_values
        )
        r.gelu[b] = gelu
        r.slope[b] = up_values * slope
        active = (gelu * up_values).astype(bf16)
        r.active[128 * b : 128 * b + 128, :] = active
        r.part_b[b] = dot(active, w_down, 1, 1).astype(bf16)
    dense = sum_rows(r.part_b, r.got_b, r.passed_b, r.far_b)
    middle = r.middle[...]
    cotangent = r.cotangent[...].astype(f32)
    dv, grad_end = norm_parts(dense, cotangent, gain_end, width)

    def finish_out():
        layer = middle + dense * inverse_scale(dense, width) * gain_end
        r.layer_out[...] = layer.astype(bf16)

    gather_rows(r.grad_dense, dv.astype(bf16), finish_out)
    for b in range(4):
        rows = slice(128 * b, 128 * b + 128)
        grad_active = dot(r.grad_dense[b], w_down, 1, 0)
        grad_gate = (grad_active * r.slope[b]).astype(bf16)
        grad_up = (grad_active * r.gelu[b]).astype(bf16)
        r.grad_gate[rows, :] = grad_gate
        r.grad_up[rows, :] = grad_up
        r.part_c[b] = (dot(grad_gate, w_gate, 1, 1) + dot(grad_up, w_up, 1, 1)).astype(bf16)

    def weight_grad(name, left, right):
        grads = getattr(r, "g_" + name)
        grads[...] = dot(left, right, 0, 0).astype(bf16).reshape(grads.shape)
        collect_on(name)

    def rows_of(ref):
        return ref[...].reshape(512, ref.shape[2])

    def down_grad():
        weight_grad("down", rows_of(r.grad_dense), r.active[...])

    def gate_grad():
        weight_grad("gate", rows_of(r.mixed), r.grad_gate[...])
        collect_on("down")

    def up_grad():
        weight_grad("up", rows_of(r.mixed), r.grad_up[...])
        collect_on("down", "gate")

    grad_mixed = sum_rows(r.part_c, r.got_c, r.passed_c, r.far_c, (down_grad, gate_grad))
    dv, grad_mid = norm_parts(middle, grad_mixed, gain_mid, width)
    grad_middle = cotangent + dv
    r.grad_middle[...] = grad_middle
    dv, grad_post = norm_parts(r.attended[...], grad_middle, gain_post, width)
    gather_rows(r.grad_attended, dv.astype(bf16), up_grad)

    r.grad_keys[...] = jnp.zeros_like(r.grad_keys)
    r.grad_values[...] = jnp.zeros_like(r.grad_values)
    grad_qgain = jnp.zeros((1, HD), f32)
    for b in range(4):
        window = slice(128 * b, 128 * b + 128 + WINDOW)
        rows = slice(128 * b, 128 * b + 128)
        grad_context = dot(r.grad_attended[b], w_project, 1, 0).astype(bf16)
        weights = r.weights[b]
        grad_probs = dot(grad_context, r.values[window, :], 1, 1)
        inner = jnp.sum(weights * grad_probs, axis=-1, keepdims=True)
        grad_scores = (weights * (grad_probs - inner)).astype(bf16)
        grad_query = dot(grad_scores, r.keys[window, :], 1, 0) * score_scale
        r.grad_keys[window, :] += dot(grad_scores, r.queries[b], 0, 0)
        r.grad_values[window, :] += dot(weights.astype(bf16), grad_context, 0, 0)
        w = rotate_back(grad_query, r.cos[4 + b], r.sin[4 + b])
        dv, dg = norm_parts(r.query_pre[b], w, gain_query, HD)
        grad_qgain = grad_qgain + dg
        grad_query_low = dv.astype(bf16)
        r.grad_query[rows, :] = grad_query_low
        if b % 2 == 1:
            collect_on(*LATE)

    def key_back(b, grad_kgain):
        place = pl.ds(pl.multiple_of(b * 128, 128), 128)
        w = rotate_back(r.grad_keys[place, :] * score_scale, r.cos[b], r.sin[b])
        dv, dg = norm_parts(r.key_pre[b], w, gain_key, HD)
        r.key_low[place, :] = dv.astype(bf16)
        r.value_low[place, :] = r.grad_values[place, :].astype(bf16)
        return grad_kgain + dg

    grad_kgain = lax.fori_loop(0, 8, key_back, jnp.zeros((1, HD), f32))
    normed_ext = r.normed[...].reshape(1024, wide)
    weight_grad("key", normed_ext, r.key_low[...])
    weight_grad("value", normed_ext, r.value_low[...])
    for b in range(4):
        prev, rows = slice(128 * b, 128 * b + 128), slice(512 + 128 * b, 640 + 128 * b)
        r.part_d[b, :, wide:] = (
            dot(r.key_low[prev, :], w_key, 1, 1) + dot(r.value_low[prev, :], w_value, 1, 1)
        ).astype(bf16)
        r.part_d[b, :, :wide] = (
            dot(r.grad_query[prev, :], w_query, 1, 1)
            + dot(r.key_low[rows, :], w_key, 1, 1)
            + dot(r.value_low[rows, :], w_value, 1, 1)
        ).astype(bf16)

    def query_grad():
        weight_grad("query", r.normed[4:8].reshape(512, wide), r.grad_query[...])
        collect_on(*SHARED)

    def project_grad():
        weight_grad("project", rows_of(r.grad_attended), rows_of(r.context))
        collect_on(*SHARED, *LATE)

    total = sum_rows(r.part_d, r.got_d, r.passed_d, r.far_d, (query_grad, project_grad))
    r.low[...] = total[:, wide:].astype(bf16)
    back = start(r.low, r.landed, dict(fsdp=before))
    collect_on(*SHARED, *NEXT)
    back.wait_recv()
    keep = (f < n - 1).astype(f32)
    grad_normed = total[:, :wide] + r.landed[...].astype(f32) * keep
    tokens = r.tokens[...].astype(f32)
    dv, grad_pre = norm_parts(tokens, grad_normed, gain_pre, width)
    r.tokens_grad[...] = (r.grad_middle[...] + dv).astype(bf16)
    row = iota((16, wide), 0)
    gain_rows = jnp.zeros((16, wide), f32)
    for k, g in enumerate((grad_pre, grad_post, grad_mid, grad_end)):
        gain_rows = jnp.where(row == k, g, gain_rows)
    row = iota((16, HD), 0)
    head_rows = jnp.where(row == 4, grad_qgain, jnp.where(row == 5, grad_kgain, 0.0))
    gain_rows, head_rows = gain_rows.astype(bf16), head_rows.astype(bf16)
    each = wide // n

    def piece(columns, k, size):
        c, lane = iota((columns, 128), 0), iota((columns, 128), 1)
        return ((c == lane + k * size) & (lane < size)).astype(bf16)

    def cut(k, carry):
        laid = dot(gain_rows, piece(wide, k, each), 1, 0)
        laid = laid + dot(head_rows, piece(HD, k, small), 1, 0)
        r.g_extra[k] = laid.astype(bf16)
        return carry

    lax.fori_loop(0, n, cut, 0)
    extra_copies = []
    for k, device in enumerate(others):
        copy = remote(
            r.g_extra.at[device],
            r.land_extra.at[k],
            (r.sum_send.at[7], r.sum_recv.at[7]),
            k,
            dict(fsdp=device),
        )
        copy.start()
        extra_copies.append(copy)
    order = SHARED + NEXT
    for s in range(n - 1):
        collect_on(*order)
    tp_copies = {}
    for copy in extra_copies:
        copy.wait_recv()
    extra_total = jnp.sum(r.land_extra[...].astype(f32), axis=0) + r.g_extra[f].astype(f32)
    for name in TWICE:
        total = collect[name].finish(f) if name in SHARED else extra_total
        getattr(r, "o_" + name)[...] = total
        held = getattr(r, "held_" + name)
        held[...] = total.astype(bf16)
        tp_copies[name] = [
            start(held, getattr(r, "peer_" + name).at[k], dict(tp=peer))
            for k, peer in enumerate((sib, far, opp))
        ]
    for name in NEXT:
        getattr(r, "o_" + name)[...] = collect[name].finish(f)
    for name in TWICE:
        for copy in tp_copies[name]:
            copy.wait_recv()
        out, peer = getattr(r, "o_" + name), getattr(r, "peer_" + name)
        out[...] += peer[0].astype(f32) + peer[1].astype(f32) + peer[2].astype(f32)
    for ring in list(fetch.values()) + list(collect.values()):
        for copy in ring.sent:
            copy.wait_send()
    for copy in gain_copies + extra_copies + unsent:
        copy.wait_send()


def hand_over_kernel(count, *refs):
    for k in range(count):
        value = refs[k][...]
        out = refs[count + k]
        out[...] = value


def hand_over(arrays):
    return pl.pallas_call(
        functools.partial(hand_over_kernel, len(arrays)),
        out_shape=[jax.ShapeDtypeStruct(a.shape, a.dtype) for a in arrays],
        in_specs=[VMEM] * len(arrays),
        out_specs=[VMEM] * len(arrays),
        compiler_params=pltpu.CompilerParams(vmem_limit_bytes=VMEM_LIMIT),
    )(*arrays)


def run_layer(n, width, small, inputs):
    shapes = {name: ref.shape for name, ref in inputs.items()}
    rows, wide = shapes["tokens"]
    dma = pltpu.SemaphoreType.DMA
    outs = dict(
        layer_out=jax.ShapeDtypeStruct((rows, wide), bf16),
        tokens_grad=jax.ShapeDtypeStruct((rows, wide), bf16),
    )
    piece = {name: shapes["s_" + name] for name in WEIGHTS}
    piece["extra"] = shapes["gains"]
    for name in SUM_WAY:
        outs["o_" + name] = jax.ShapeDtypeStruct(piece[name], f32)
    group = (4, rows, wide)
    hidden = piece["gate"][1]
    scratch = dict(
        all_gains=((n, *shapes["gains"]), bf16),
        marks=((4, *shapes["places"]), jnp.int32),
        normed=((8, rows, wide), bf16),
        key_pre=((8, rows, HD), f32),
        query_pre=((4, rows, HD), f32),
        queries=((4, rows, HD), bf16),
        keys=((8 * rows, HD), bf16),
        values=((8 * rows, HD), bf16),
        weights=((4, rows, rows + WINDOW), f32),
        context=((4, rows, HD), bf16),
        attended=((rows, wide), f32),
        middle=((rows, wide), f32),
        grad_middle=((rows, wide), f32),
        mixed=(group, bf16),
        grad_dense=(group, bf16),
        grad_attended=(group, bf16),
        gelu=((4, rows, hidden), f32),
        slope=((4, rows, hidden), f32),
        active=((4 * rows, hidden), bf16),
        grad_gate=((4 * rows, hidden), bf16),
        grad_up=((4 * rows, hidden), bf16),
        grad_keys=((8 * rows, HD), f32),
        grad_values=((8 * rows, HD), f32),
        grad_query=((4 * rows, HD), bf16),
        low=((rows, wide), bf16),
        landed=((rows, wide), bf16),
        key_low=((8 * rows, HD), bf16),
        value_low=((8 * rows, HD), bf16),
    )
    for tag in "abcd":
        across = 2 * wide if tag == "d" else wide
        scratch["part_" + tag] = ((4, rows, across), bf16)
        scratch["got_" + tag] = ((2, rows, across), bf16)
        scratch["passed_" + tag] = ((rows, across), bf16)
        scratch["far_" + tag] = ((rows, across), bf16)
    for name in WEIGHTS:
        scratch["w_" + name] = ((n, *piece[name]), bf16)
    for name in SUM_WAY:
        scratch["g_" + name] = ((n, *piece[name]), bf16)
        scratch["land_" + name] = ((n - 1, *piece[name]), bf16)
    for name in TWICE:
        scratch["held_" + name] = (piece[name], bf16)
        scratch["peer_" + name] = ((3, *piece[name]), bf16)
    sems = dict(
        local_sem=(9,),
        gain_send=(n - 1,),
        gain_recv=(n - 1,),
        tp_send=(48,),
        tp_recv=(48,),
        fetch_send=(7, n - 1),
        fetch_recv=(7, n - 1),
        sum_send=(8, n - 1),
        sum_recv=(8, n - 1),
    )
    names = [*inputs, *outs, *scratch, *sems]
    results = pl.pallas_call(
        functools.partial(layer_kernel, n, width, small, names),
        out_shape=list(outs.values()),
        in_specs=[VMEM] * len(inputs),
        out_specs=[VMEM] * len(outs),
        scratch_shapes=[pltpu.VMEM(*s) for s in scratch.values()]
        + [dma(s) for s in sems.values()],
        compiler_params=params(1),
    )(*inputs.values())
    return dict(zip(outs, results))


def per_device(
    n,
    tokens,
    sequence_ids,
    positions,
    query_weight,
    key_weight,
    value_weight,
    project_weight,
    gate_weight,
    up_weight,
    down_weight,
    prenorm,
    postnorm,
    midnorm,
    endnorm,
    querynorm,
    keynorm,
    cotangent,
):
    rows, width = tokens.shape
    part = query_weight.shape[0]
    padded = -(-part // 16) * 16
    small = querynorm.shape[0]

    def pad_rows(a):
        return jnp.pad(a, ((0, padded - part), (0, 0))) if part < padded else a

    def pad_wide(a):
        if part == padded:
            return a
        a = jnp.pad(a.reshape(rows, n, part), ((0, 0), (0, 0), (0, padded - part)))
        return a.reshape(rows, n * padded)

    def cut_wide(a):
        if part == padded:
            return a
        return a.reshape(rows, n, padded)[:, :, :part].reshape(rows, width)

    gains = [jnp.pad(g, (0, 128 - part)) for g in (prenorm, postnorm, midnorm, endnorm)]
    gains += [jnp.pad(g, (0, 128 - small)) for g in (querynorm, keynorm)]
    half = HD // 2
    frequency = rope_base ** (-2.0 * np.arange(half) / HD)
    angles = np.arange(8 * rows)[:, None] * frequency[None, :]
    cos, sin = (np.asarray(a, np.float32).reshape(8, rows, half) for a in (np.cos(angles), np.sin(angles)))
    inputs = dict(
        tokens=pad_wide(tokens),
        cotangent=pad_wide(cotangent),
        places=jnp.broadcast_to(positions[None, :], (8, rows)),
        gains=jnp.pad(jnp.stack(gains), ((0, 10), (0, 0))),
        cos=jnp.asarray(cos),
        sin=jnp.asarray(sin),
        s_query=pad_rows(query_weight),
        s_key=pad_rows(key_weight),
        s_value=pad_rows(value_weight),
        s_project=pad_rows(project_weight.T),
        s_gate=pad_rows(gate_weight),
        s_up=pad_rows(up_weight),
        s_down=pad_rows(down_weight.T),
    )
    out = run_layer(n, width, small, inputs)
    (
        layer_out,
        tokens_grad,
        s_query,
        s_key,
        s_value,
        s_project,
        s_gate,
        s_up,
        s_down,
        extra,
    ) = hand_over(
        [
            out["layer_out"],
            out["tokens_grad"],
            out["o_query"],
            out["o_key"],
            out["o_value"],
            out["o_project"],
            out["o_gate"],
            out["o_up"],
            out["o_down"],
            out["o_extra"],
        ],
    )
    return (
        cut_wide(layer_out),
        cut_wide(tokens_grad),
        s_query[:part],
        s_key[:part],
        s_value[:part],
        s_project[:part].T,
        s_gate[:part],
        s_up[:part],
        s_down[:part].T,
        *[extra[k, :part] for k in range(4)],
        *[extra[k, :small] for k in (4, 5)],
    )


def solution(mesh):
    rows = P(("fsdp", "tp"), None)
    marks = P(("fsdp", "tp"))
    both, down, across, gain = P("fsdp", "tp"), P("fsdp", None), P("tp", "fsdp"), P("fsdp")
    return jax.shard_map(
        functools.partial(per_device, mesh.shape["fsdp"]),
        mesh=mesh,
        in_specs=(rows, marks, marks, both, down, down, across, both, both, across)
        + (gain,) * 6
        + (rows,),
        out_specs=(rows, rows, both, down, down, across, both, both, across) + (gain,) * 6,
        check_vma=False,
    )
```
